512 devices in a mesh: dp: 16 (over z_hi, x, core), ctx: 32 (over y, z_lo).
Axes of the slice: x: 4, y: 8, z: 8 (z_hi: 2, z_lo: 4; z = z_hi * 4 + z_lo), core: 2. Of those that a mesh axis runs over, the one named last changes fastest.
Arguments:
- inputs: bfloat16 [16, 4096, 8192], P('dp', 'ctx'), may hold values from -6 to 6
- queries: bfloat16 [16, 4096, 4096], P('dp', 'ctx'), may hold values from -48 to 48
- upstream: bfloat16 [16, 4096, 4096], P('dp', 'ctx'), may hold values from -6 to 6
- lengths: int32 [16, 32], P('dp'), may hold values from 1 to 384, 4096 in all within a row
- factor_k: bfloat16 [2048, 4, 128], P('ctx'), may hold values from -0.0625 to 0.0625
- factor_v: bfloat16 [2048, 4, 128], P('ctx'), may hold values from -0.0625 to 0.0625
- mixing_k: float32 [4, 4, 4], replicated, may hold values from -3 to 3
- mixing_v: float32 [4, 4, 4], replicated, may hold values from -3 to 3
Outputs:
- grad_factor_k: float32 [2048, 4, 128], P('ctx')
- grad_factor_v: float32 [2048, 4, 128], P('ctx')
- grad_mixing_k: float32 [4, 4, 4], replicated
- grad_mixing_v: float32 [4, 4, 4], replicated
The draws below stay inside these ranges and needn't reach their ends.
Inputs may be any that keep to these rules, and one draw needn't show every extreme that they name: Each row holds 32 document lengths that sum to 4096; the longest is exactly 384.
All inputs are finite; a program needn't handle non-finite values.
Results may differ from the reference program's by a relative error of at most 0.03.
The reference program's roundings to bfloat16 on the way (of `probs_b` and `dscores`) count: a program that leaves them out, or rounds other values in their place, can miss the bound.
Values may be sent and summed in bfloat16 or wider, within the bound.
No kernel may reach another device: no remote copies, remote signals or barrier semaphores. Data moves between devices by JAX's collectives and lax.ppermute only.
A program may use at most 64 MiB of HBM per device.

```python
import math
import jax
import jax.numpy as jnp
import numpy as np
from jax import lax

D = 8192
HEADS = 32
KVH = 4
HD = 128
NPHM = 4
REACH = 3
TOK_DEV = 128
GROUP = 8
E = 512
DQ = 2048
EQ = 128
SEQ = 4096
SEQS = 16
NDOC = 32
N_CTX = 32


def draw_queries(key, part):
    first = jax.random.fold_in(key, 0)
    base = jax.random.truncated_normal(first, -6.0, 6.0, (SEQS, SEQ, HEADS * HD), jnp.float32)
    return base.astype(jnp.bfloat16)


def level_of(rng, shape, pieces, smallest, high):
    def one(axis_at, shards_of):
        heights = jax.random.uniform(jax.random.fold_in(jax.random.fold_in(rng, 6), axis_at), (shards_of,), jnp.float32, smallest / len(pieces), high / len(pieces))
        return jnp.repeat(jnp.exp(heights), shape[axis_at] // shards_of).reshape((-1,) + (1,) * (len(shape) - axis_at - 1))

    factor_of = one(*pieces[0])
    for cut in pieces[1:]:
        factor_of = factor_of * one(*cut)
    return factor_of


def split_up(number_of, total, reach, slope):
    weights = [(1 << 20) // math.isqrt(standing ** slope) + 1 for standing in range(2, number_of + 1)]
    spare, given = total - reach - (number_of - 1), [1] * (number_of - 1)
    while spare > 0:
        movable = [i for i in range(number_of - 1) if given[i] < reach]
        mass, budget = sum([weights[i] for i in movable]), spare
        for i in movable:
            extra = min(reach - given[i], max(1, budget * weights[i] // mass), spare)
            given[i] = given[i] + extra
            spare = spare - extra
    return np.array([reach] + given)


def ragged_sizes(key, amount, total, bound, skew):
    if amount == 2:
        one = jax.random.randint(key, (), max(1, total - bound), min(bound, total - 1) + 1)
        return jnp.stack([one, total - one])
    sizes = jnp.asarray(split_up(amount, total, bound, skew), jnp.int32)
    pairs = (amount - 1) // 2
    source_of, sink = sizes[1:1 + 2 * pairs:2], sizes[2:2 + 2 * pairs:2]
    slack = jnp.minimum(source_of - 1, bound - sink)
    shifted = jax.random.randint(jax.random.fold_in(key, 1), (pairs,), 0, 1 << 20) % (slack + 1)
    sizes = sizes.at[1:1 + 2 * pairs:2].set(source_of - shifted).at[2:2 + 2 * pairs:2].set(sink + shifted)
    return sizes[jax.random.permutation(jax.random.fold_in(key, 2), amount)]


def gaussian(key, extent, scale, reach, pieces=(), held_as=jnp.bfloat16):
    entries = jax.random.normal(key, extent, jnp.float32) * scale
    if len(pieces) > 0:
        entries = level_of(key, extent, pieces, -0.22, 0.18) * entries
    return jnp.clip(entries, min=-reach, max=reach).astype(held_as)


def setup_inputs(seed: int = 0) -> dict:
    key_list = jax.random.split(jax.random.key(seed), 9)
    return {
        "inputs": gaussian(key_list[0], (SEQS, SEQ, D), 1.0, 6.0, ((0, 16), (1, 32))),
        "queries": draw_queries(jax.random.fold_in(key_list[8], 71), 0),
        "upstream": gaussian(key_list[2], (SEQS, SEQ, HEADS * HD), 1.0, 6.0, ((0, 16), (1, 32))),
        "lengths": jax.vmap(lambda own: ragged_sizes(own, NDOC, SEQ, 3 * TOK_DEV, 2))(jax.random.split(key_list[3], SEQS)).reshape((SEQS, NDOC)).astype(jnp.int32),
        "factor_k": gaussian(key_list[4], (DQ, NPHM, EQ), D ** -0.5, 0.0625, ((0, 32),)),
        "factor_v": gaussian(key_list[5], (DQ, NPHM, EQ), D ** -0.5, 0.0625, ((0, 32),)),
        "mixing_k": gaussian(key_list[6], (NPHM, NPHM, NPHM), 0.5, 3.0, (), jnp.float32),
        "mixing_v": gaussian(key_list[7], (NPHM, NPHM, NPHM), 0.5, 3.0, (), jnp.float32),
    }


def group_grads(qg, dog, kg, vg, mask, scale):
    qf = qg.astype(jnp.float32)
    dof = dog.astype(jnp.float32)
    scores = jnp.einsum('trd,sd->rts', qf, kg.astype(jnp.float32)) * scale
    scores = jnp.where(mask[None], scores, -1e+30)
    top = lax.optimization_barrier(jnp.max(scores, axis=-1, keepdims=True))
    weights = jnp.exp(scores - top)
    probs = weights / lax.optimization_barrier(jnp.sum(weights, axis=-1, keepdims=True))
    probs_b = probs.astype(jnp.bfloat16).astype(jnp.float32)
    grad_v = jnp.einsum('rts,trd->sd', probs_b, dof)
    dprobs = jnp.einsum('trd,sd->rts', dof, vg.astype(jnp.float32))
    delta = lax.optimization_barrier(jnp.sum(probs * dprobs, axis=-1, keepdims=True))
    dscores = (probs * (dprobs - delta)).astype(jnp.bfloat16).astype(jnp.float32)
    grad_k = jnp.einsum('rts,trd->sd', dscores, qf) * scale
    return (grad_k, grad_v)

def one_sequence(inputs, queries, upstream, lengths, factor_k, factor_v, mixing_k, mixing_v):
    hi = lax.Precision.HIGHEST
    x4 = inputs.reshape(SEQ, NPHM, DQ).astype(jnp.float32)
    part_k = jnp.einsum('tap,piq->itaq', x4, factor_k.astype(jnp.float32))
    part_v = jnp.einsum('tap,piq->itaq', x4, factor_v.astype(jnp.float32))
    keys = jnp.einsum('iab,itaq->tbq', mixing_k, part_k, precision=hi).reshape(SEQ, E).astype(jnp.bfloat16)
    values = jnp.einsum('iab,itaq->tbq', mixing_v, part_v, precision=hi).reshape(SEQ, E).astype(jnp.bfloat16)
    ends = jnp.cumsum(lengths).astype(jnp.int32)
    pos = jnp.arange(SEQ, dtype=jnp.int32)
    docs = lax.optimization_barrier(jnp.sum((ends[None, :] <= pos[:, None]).astype(jnp.int32), axis=1)).astype(jnp.int32)
    front = REACH * TOK_DEV
    win = (REACH + 1) * TOK_DEV
    keys_pad = jnp.concatenate([jnp.zeros((front, E), jnp.bfloat16), keys], axis=0)
    values_pad = jnp.concatenate([jnp.zeros((front, E), jnp.bfloat16), values], axis=0)
    docs_pad = jnp.concatenate([jnp.full((front,), -1, jnp.int32), docs], axis=0)
    scale = 1.0 / math.sqrt(HD)

    def run(carry, index):
        gk_pad, gv_pad = carry
        start = (index * TOK_DEV).astype(jnp.int32)
        q_run = lax.dynamic_slice_in_dim(queries, start, TOK_DEV, 0)
        d_run = lax.dynamic_slice_in_dim(upstream, start, TOK_DEV, 0)
        k_win = lax.dynamic_slice_in_dim(keys_pad, start, win, 0)
        v_win = lax.dynamic_slice_in_dim(values_pad, start, win, 0)
        kdoc = lax.dynamic_slice_in_dim(docs_pad, start, win, 0)
        qdoc = lax.dynamic_slice_in_dim(docs, start, TOK_DEV, 0)
        qpos = start + jnp.arange(TOK_DEV, dtype=jnp.int32)
        kpos = start - front + jnp.arange(win, dtype=jnp.int32)
        mask = (kpos[None, :] <= qpos[:, None]) & (kpos[None, :] >= 0) & (kdoc[None, :] == qdoc[:, None])
        qg = q_run.reshape(TOK_DEV, KVH, GROUP, HD).transpose(1, 0, 2, 3)
        dg = d_run.reshape(TOK_DEV, KVH, GROUP, HD).transpose(1, 0, 2, 3)
        kg = k_win.reshape(win, KVH, HD).transpose(1, 0, 2)
        vg = v_win.reshape(win, KVH, HD).transpose(1, 0, 2)
        grad_k, grad_v = lax.map(lambda item: group_grads(item[0], item[1], item[2], item[3], mask, scale), (qg, dg, kg, vg))
        grad_k = grad_k.transpose(1, 0, 2).reshape(win, E)
        grad_v = grad_v.transpose(1, 0, 2).reshape(win, E)
        gk_pad = lax.dynamic_update_slice_in_dim(gk_pad, lax.dynamic_slice_in_dim(gk_pad, start, win, 0) + grad_k, start, 0)
        gv_pad = lax.dynamic_update_slice_in_dim(gv_pad, lax.dynamic_slice_in_dim(gv_pad, start, win, 0) + grad_v, start, 0)
        return ((gk_pad, gv_pad), None)
    zero_pad = jnp.zeros((SEQ + front, E), jnp.float32)
    (gk_pad, gv_pad), _ = lax.scan(run, (zero_pad, zero_pad), jnp.arange(N_CTX, dtype=jnp.int32))
    grad_keys_b = gk_pad[front:].astype(jnp.bfloat16).astype(jnp.float32).reshape(SEQ, NPHM, EQ)
    grad_values_b = gv_pad[front:].astype(jnp.bfloat16).astype(jnp.float32).reshape(SEQ, NPHM, EQ)
    mixed_k = jnp.einsum('iab,tbq->itaq', mixing_k, grad_keys_b, precision=hi).astype(jnp.bfloat16).astype(jnp.float32)
    mixed_v = jnp.einsum('iab,tbq->itaq', mixing_v, grad_values_b, precision=hi).astype(jnp.bfloat16).astype(jnp.float32)

    def factor_run(carry, index):
        start = (index * TOK_DEV).astype(jnp.int32)
        x_run = lax.dynamic_slice_in_dim(x4, start, TOK_DEV, 0)
        mk = lax.dynamic_slice_in_dim(mixed_k, start, TOK_DEV, 1)
        mv = lax.dynamic_slice_in_dim(mixed_v, start, TOK_DEV, 1)
        term_k = jnp.einsum('tap,itaq->piq', x_run, mk).astype(jnp.bfloat16)
        term_v = jnp.einsum('tap,itaq->piq', x_run, mv).astype(jnp.bfloat16)
        term_k, term_v = lax.optimization_barrier((term_k, term_v))
        return ((carry[0] + term_k.astype(jnp.float32), carry[1] + term_v.astype(jnp.float32)), None)
    zero_f = jnp.zeros((DQ, NPHM, EQ), jnp.float32)
    (grad_fk, grad_fv), _ = lax.scan(factor_run, (zero_f, zero_f), jnp.arange(N_CTX, dtype=jnp.int32))
    grad_mk = jnp.einsum('itaq,tbq->iab', part_k, grad_keys_b, precision=hi)
    grad_mv = jnp.einsum('itaq,tbq->iab', part_v, grad_values_b, precision=hi)
    return (grad_fk, grad_fv, grad_mk, grad_mv)

def reference(inputs, queries, upstream, lengths, factor_k, factor_v, mixing_k, mixing_v):

    def single(item):
        return one_sequence(item[0], item[1], item[2], item[3], factor_k, factor_v, mixing_k, mixing_v)
    grad_fk, grad_fv, grad_mk, grad_mv = lax.map(single, (inputs, queries, upstream, lengths))
    return (lax.optimization_barrier(jnp.sum(grad_fk, axis=0)), lax.optimization_barrier(jnp.sum(grad_fv, axis=0)), lax.optimization_barrier(jnp.sum(grad_mk, axis=0)), lax.optimization_barrier(jnp.sum(grad_mv, axis=0)))
```

```python
import functools
import math

import jax
import jax.numpy as jnp
from jax import lax
from jax.experimental import pallas as pl
from jax.experimental.pallas import tpu as pltpu
from jax.sharding import Mesh, PartitionSpec as P

KVH = 4
HD = 128
REACH = 3
GROUP = 8
NPHM = 4
PAD = 16
CTX = ("y", "zl")
DP = ("zh", "x", "c")
SCALE = 1.0 / math.sqrt(HD)
LOG2E = 1.4426950408889634
SMEM = pl.BlockSpec(memory_space=pltpu.SMEM)
F32 = jnp.float32
BF16 = jnp.bfloat16


def dot(a, b, ca, cb):
    return lax.dot_general(a, b, (((ca,), (cb,)), ((), ())), preferred_element_type=F32)


def params(mib):
    return pltpu.CompilerParams(vmem_limit_bytes=mib << 20)


def project_kernel(mix, xm, xo, w, part, out, wide, acc):
    a = pl.program_id(0)

    @pl.when(a == 0)
    def _():
        for i in range(NPHM):
            wide[:, i * HD : (i + 1) * HD] = w[i]
        acc[...] = jnp.zeros_like(acc)

    x = jnp.concatenate([xm[0], xo[0]], axis=0)
    one = dot(x, wide[...], 1, 0)
    part[0] = one
    for b in range(NPHM):
        at = slice(b * HD, (b + 1) * HD)
        total = acc[:, at]
        for i in range(NPHM):
            total = total + mix[i * 16 + a * 4 + b] * one[:, i * HD : (i + 1) * HD]
        acc[:, at] = total

    @pl.when(a == NPHM - 1)
    def _():
        tok = xm.shape[1]
        out[0] = acc[:tok].astype(BF16)
        out[1] = acc[tok:].astype(BF16)


def project(mix, xm, xo, w):
    tok, width = xm.shape[1:]
    dq, cols = width // NPHM, NPHM * HD
    return pl.pallas_call(
        project_kernel,
        grid=(NPHM,),
        in_specs=[
            SMEM,
            pl.BlockSpec((1, tok, dq), lambda a: (0, 0, a)),
            pl.BlockSpec((1, tok, dq), lambda a: (0, 0, a)),
            pl.BlockSpec((NPHM, dq, HD), lambda a: (0, 0, 0)),
        ],
        out_specs=[
            pl.BlockSpec((1, 2 * tok, cols), lambda a: (a, 0, 0)),
            pl.BlockSpec((2, tok, cols), lambda a: (0, 0, 0)),
        ],
        out_shape=[
            jax.ShapeDtypeStruct((NPHM, 2 * tok, cols), F32),
            jax.ShapeDtypeStruct((2, tok, cols), BF16),
        ],
        scratch_shapes=[pltpu.VMEM((dq, cols), BF16), pltpu.VMEM((2 * tok, cols), F32)],
        compiler_params=params(40),
    )(mix, xm, xo, w)


def attend_kernel(base, lens, q, do, w3, w2, w1, w0, s3, s2, s1, own, bias, probs, dscores):
    tok = q.shape[1]
    win = (REACH + 1) * tok

    @pl.when(pl.program_id(0) == 0)
    def _():
        start = base[0]
        qpos = start + lax.broadcasted_iota(jnp.int32, (8, tok), 1)

        def step(n, carry):
            end, first = carry
            end = end + lens[n]
            return end, jnp.where(end <= qpos, end, first)

        _, first = lax.fori_loop(
            0, lens.shape[0], step, (jnp.int32(0), jnp.zeros((8, tok), jnp.int32))
        )
        kpos = start - REACH * tok + lax.broadcasted_iota(jnp.int32, (win, tok), 0)
        ok = (kpos >= first[0:1]) & (kpos <= qpos[0:1])
        bias[...] = jnp.where(ok, 0.0, -1e30).astype(F32)

    k = jnp.concatenate([w[0] for w in (w3, w2, w1, w0)], axis=0)
    v = jnp.concatenate([w[1] for w in (w3, w2, w1, w0)], axis=0)
    for r in range(GROUP):
        at = slice(r * HD, (r + 1) * HD)
        rows = slice(r * tok, (r + 1) * tok)
        s = dot(k, q[0, :, at], 1, 1) * (SCALE * LOG2E) + bias[...]
        dp = dot(v, do[0, :, at], 1, 1)
        e = jnp.exp2(s - jnp.max(s, axis=0, keepdims=True))
        p = e * (1.0 / jnp.sum(e, axis=0, keepdims=True))
        delta = jnp.sum(p * dp, axis=0, keepdims=True)
        probs[:, rows] = p.astype(BF16)
        dscores[:, rows] = (p * (dp - delta)).astype(BF16)
    qs = jnp.concatenate([q[0, :, r * HD : (r + 1) * HD] for r in range(GROUP)], axis=0)
    dos = jnp.concatenate([do[0, :, r * HD : (r + 1) * HD] for r in range(GROUP)], axis=0)
    gk = dot(dscores[...], qs, 1, 0) * SCALE
    gv = dot(probs[...], dos, 1, 0)
    for n, out in enumerate((s3, s2, s1)):
        out[0] = gk[n * tok : (n + 1) * tok].astype(BF16)
        out[1] = gv[n * tok : (n + 1) * tok].astype(BF16)
    own[0] = gk[REACH * tok :]
    own[1] = gv[REACH * tok :]


def attend(base, lens, q, do, wins):
    tok = q.shape[1]
    win = (REACH + 1) * tok
    wide = GROUP * HD
    head = pl.BlockSpec((1, tok, wide), lambda g: (0, 0, g))
    run = pl.BlockSpec((2, tok, HD), lambda g: (0, 0, g))
    shape = (2, tok, KVH * HD)
    return pl.pallas_call(
        attend_kernel,
        grid=(KVH,),
        in_specs=[SMEM, SMEM, head, head] + [run] * 4,
        out_specs=[run] * 4,
        out_shape=[jax.ShapeDtypeStruct(shape, BF16)] * 3 + [jax.ShapeDtypeStruct(shape, F32)],
        scratch_shapes=[
            pltpu.VMEM((win, tok), F32),
            pltpu.VMEM((win, GROUP * tok), BF16),
            pltpu.VMEM((win, GROUP * tok), BF16),
        ],
        compiler_params=params(40),
    )(base, lens, q, do, *wins)


def factor_kernel(mix, *refs):
    xs, (gm, go, part, out, row, mixed, grads) = refs[:8], refs[8:]
    j = pl.program_id(0)
    tok = gm.shape[0]

    @pl.when(j == 0)
    def _():
        grads[:tok] = gm[...].astype(F32)
        grads[tok:] = go[...].astype(F32)
        for a in range(NPHM):
            for i in range(NPHM):
                total = mix[i * 16 + a * 4] * grads[:, :HD]
                for b in range(1, NPHM):
                    total = total + mix[i * 16 + a * 4 + b] * grads[:, b * HD : (b + 1) * HD]
                mixed[a, :, i * HD : (i + 1) * HD] = total.astype(BF16)
        sums = []
        for i in range(NPHM):
            for a in range(NPHM):
                for b in range(NPHM):
                    both = part[a, :, i * HD : (i + 1) * HD] * grads[:, b * HD : (b + 1) * HD]
                    sums.append(jnp.sum(both, axis=0, keepdims=True))
        sums = jnp.sum(jnp.concatenate(sums, axis=0), axis=1, keepdims=True)
        many = NPHM**3
        spot = lax.broadcasted_iota(jnp.int32, (many, 2 * many), 0)
        lane = lax.broadcasted_iota(jnp.int32, (many, 2 * many), 1)
        line = jnp.sum(jnp.where(spot == lane, sums, 0.0), axis=0, keepdims=True)
        row[...] = jnp.broadcast_to(line, row.shape)

    total = None
    for a in range(NPHM):
        x = jnp.concatenate([xs[a][0], xs[4 + a][0]], axis=0)
        one = dot(mixed[a], x, 0, 0)
        total = one if total is None else total + one
    for i in range(NPHM):
        out[i] = total[i * HD : (i + 1) * HD].astype(BF16)


def factor_grads(mix, xm, xo, gm, go, part):
    tok, width = xm.shape[1:]
    dq, cols = width // NPHM, NPHM * HD
    steps = 4
    wide = dq // steps
    xspecs = [
        pl.BlockSpec((1, tok, wide), functools.partial(lambda a, j: (0, 0, a * steps + j), a))
        for a in range(NPHM)
    ]
    whole = pl.BlockSpec((tok, cols), lambda j: (0, 0))
    return pl.pallas_call(
        factor_kernel,
        grid=(steps,),
        in_specs=[SMEM]
        + xspecs
        + xspecs
        + [whole, whole, pl.BlockSpec((NPHM, 2 * tok, cols), lambda j: (0, 0, 0))],
        out_specs=[
            pl.BlockSpec((NPHM, HD, wide), lambda j: (0, 0, j)),
            pl.BlockSpec((8, HD), lambda j: (0, 0)),
        ],
        out_shape=[
            jax.ShapeDtypeStruct((NPHM, HD, dq), BF16),
            jax.ShapeDtypeStruct((8, HD), F32),
        ],
        scratch_shapes=[
            pltpu.VMEM((NPHM, 2 * tok, cols), BF16),
            pltpu.VMEM((2 * tok, cols), F32),
        ],
        compiler_params=params(40),
    )(mix, *([xm] * 4), *([xo] * 4), gm, go, part)


def split_line(value):
    lane = lax.broadcasted_iota(jnp.int32, value.shape, 1)
    high = value.astype(BF16).astype(F32)
    return jnp.where(lane < HD // 2, high, value - high)


def turn_kernel(terms, row, out):
    n, rows = out.shape[0], out.shape[1] - PAD
    total = terms[0].astype(F32)
    for i in range(1, NPHM):
        total = total + terms[i].astype(F32)
    turned = total.T.astype(BF16)
    line = row[0:1]
    line = line + jnp.concatenate([line[:, HD // 2 :], line[:, : HD // 2]], axis=1)
    line = jnp.broadcast_to(split_line(line), (PAD, HD)).astype(BF16)
    for d in range(n):
        out[d, :rows] = turned[d * rows : (d + 1) * rows]
        out[d, rows:] = line


def turn(terms, row, n):
    rows = terms.shape[2] // n
    return pl.pallas_call(
        turn_kernel,
        out_shape=jax.ShapeDtypeStruct((n, rows + PAD, HD), BF16),
        compiler_params=params(40),
    )(terms, row)


def total_kernel(blocks, out):
    rows = out.shape[1] - PAD
    total = blocks[0].astype(F32)
    for d in range(1, blocks.shape[0]):
        total = total + blocks[d].astype(F32)
    line = total[rows : rows + 1]
    line = line + jnp.concatenate([line[:, HD // 2 :], line[:, : HD // 2]], axis=1)
    line = jnp.broadcast_to(split_line(line), (PAD, HD)).astype(BF16)
    body = total[:rows].astype(BF16)
    for d in range(out.shape[0]):
        out[d, :rows] = body
        out[d, rows:] = line


def total(blocks, n):
    return pl.pallas_call(
        total_kernel,
        out_shape=jax.ShapeDtypeStruct((n,) + blocks.shape[1:], BF16),
        compiler_params=params(40),
    )(blocks)


def shards(inputs, queries, upstream, lengths, factor_k, factor_v, mixing_k, mixing_v):
    tok = inputs.shape[1]
    rows = factor_k.shape[0]
    n_ctx = lax.axis_size("y") * lax.axis_size("zl")
    n_dp = lax.axis_size("zh") * lax.axis_size("x") * lax.axis_size("c")
    ctx = lax.axis_index("y") * lax.axis_size("zl") + lax.axis_index("zl")
    x_at = lax.axis_index("x")
    first = lax.axis_index("c") == 0
    swap = [(0, 1), (1, 0)]

    other = lax.ppermute(inputs, "c", swap)
    mix = jnp.where(first, mixing_k, mixing_v).reshape(-1)
    mine = lax.dynamic_index_in_dim(
        jnp.where(first, factor_k, factor_v), x_at, axis=1, keepdims=False
    )
    piece = jnp.broadcast_to(mine[None], (n_ctx, rows, HD))
    piece = lax.all_to_all(piece, CTX, 0, 0, tiled=True).reshape(1, n_ctx * rows, HD)
    weights = lax.all_to_all(
        jnp.broadcast_to(piece, (NPHM, n_ctx * rows, HD)), "x", 0, 0, tiled=True
    )
    part, both = project(mix, inputs, other, weights)

    got = lax.ppermute(both[1], "c", swap)
    pack = jnp.stack([jnp.where(first, both[0], got), jnp.where(first, got, both[0])])
    wins = []
    for d in range(REACH, 0, -1):
        route = [(n - d, n) for n in range(d, n_ctx)]
        wins.append(lax.ppermute(pack, CTX, route))
    base = (ctx * tok).astype(jnp.int32).reshape(1)
    *away, own = attend(base, lengths[0], queries, upstream, wins + [pack])
    for d, block in zip(range(REACH, 0, -1), away):
        route = [(n, n - d) for n in range(d, n_ctx)]
        own = own + lax.ppermute(block, CTX, route).astype(F32)
    grads = own.astype(BF16)
    keep = jnp.where(first, grads[0], grads[1])
    got = lax.ppermute(jnp.where(first, grads[1], grads[0]), "c", swap)

    terms, row = factor_grads(mix, inputs, other, keep, got, part)
    terms = lax.all_to_all(terms, "x", 0, 0, tiled=True)
    blocks = lax.all_to_all(turn(terms, row, n_ctx), CTX, 0, 0, tiled=True)
    blocks = lax.all_to_all(total(blocks, n_dp), DP, 0, 0, tiled=True)
    blocks = blocks.reshape(lax.axis_size("zh"), NPHM, 2, rows + PAD, HD).astype(F32)
    blocks = jnp.sum(blocks, axis=0)
    grad_f = blocks[:, :, :rows].transpose(1, 2, 0, 3)
    lines = jnp.sum(blocks[:, :, rows], axis=0)
    lines = lines[:, : HD // 2] + lines[:, HD // 2 :]
    grad_m = lines.reshape(2, NPHM, NPHM, NPHM)
    return (grad_f[0], grad_f[1], grad_m[0], grad_m[1])


def solution(mesh):
    n_dp, n_ctx = mesh.devices.shape
    zl = 4
    shape = (n_dp // 8, 4, 2, n_ctx // zl, zl)
    wide = Mesh(mesh.devices.reshape(shape), DP + CTX)
    in_specs = (
        P(DP, CTX, None),
        P(DP, CTX, None),
        P(DP, CTX, None),
        P(DP, None),
        P(CTX, None, None),
        P(CTX, None, None),
        P(),
        P(),
    )
    out_specs = (P(CTX, None, None), P(CTX, None, None), P(), P())
    return jax.shard_map(shards, mesh=wide, in_specs=in_specs, out_specs=out_specs, check_vma=False)
```

```python
import functools
import math

import jax
import jax.numpy as jnp
from jax import lax
from jax.experimental import pallas as pl
from jax.experimental.pallas import tpu as pltpu
from jax.sharding import Mesh, PartitionSpec as P

KVH = 4
HD = 128
REACH = 3
GROUP = 8
NPHM = 4
PAD = 16
CTX = ("y", "zl")
DP = ("zh", "x", "c")
SCALE = 1.0 / math.sqrt(HD)
LOG2E = 1.4426950408889634
SMEM = pl.BlockSpec(memory_space=pltpu.SMEM)
F32 = jnp.float32
BF16 = jnp.bfloat16


def dot(a, b, ca, cb):
    return lax.dot_general(a, b, (((ca,), (cb,)), ((), ())), preferred_element_type=F32)


def around(distance):
    return [(i, (i + distance) % NPHM) for i in range(NPHM)]


def params(mib):
    return pltpu.CompilerParams(vmem_limit_bytes=mib << 20)


def project_kernel(mix, xm, xo, w, part, out, wide, acc):
    a = pl.program_id(0)

    @pl.when(a == 0)
    def _():
        for i in range(NPHM):
            wide[:, i * HD : (i + 1) * HD] = w[i]
        acc[...] = jnp.zeros_like(acc)

    x = jnp.concatenate([xm[0], xo[0]], axis=0)
    one = dot(x, wide[...], 1, 0)
    part[0] = one
    for b in range(NPHM):
        at = slice(b * HD, (b + 1) * HD)
        total = acc[:, at]
        for i in range(NPHM):
            total = total + mix[i * 16 + a * 4 + b] * one[:, i * HD : (i + 1) * HD]
        acc[:, at] = total

    @pl.when(a == NPHM - 1)
    def _():
        tok = xm.shape[1]
        for b in range(NPHM):
            done = acc[:, b * HD : (b + 1) * HD].astype(BF16)
            out[0, b] = done[:tok]
            out[1, b] = done[tok:]


def project(mix, xm, xo, w):
    tok, width = xm.shape[1:]
    dq, cols = width // NPHM, NPHM * HD
    return pl.pallas_call(
        project_kernel,
        grid=(NPHM,),
        in_specs=[
            SMEM,
            pl.BlockSpec((1, tok, dq), lambda a: (0, 0, a)),
            pl.BlockSpec((1, tok, dq), lambda a: (0, 0, a)),
            pl.BlockSpec((NPHM, dq, HD), lambda a: (0, 0, 0)),
        ],
        out_specs=[
            pl.BlockSpec((1, 2 * tok, cols), lambda a: (a, 0, 0)),
            pl.BlockSpec((2, NPHM, tok, HD), lambda a: (0, 0, 0, 0)),
        ],
        out_shape=[
            jax.ShapeDtypeStruct((NPHM, 2 * tok, cols), F32),
            jax.ShapeDtypeStruct((2, NPHM, tok, HD), BF16),
        ],
        scratch_shapes=[pltpu.VMEM((dq, cols), BF16), pltpu.VMEM((2 * tok, cols), F32)],
        compiler_params=params(40),
    )(mix, xm, xo, w)


def attend_kernel(
    where, lens, q0, q1, q2, q3, row, before, back, own, qd, keys, values, gk, gv, bias, probs, dscores
):
    tok = q0.shape[1]
    win = (REACH + 1) * tok
    o = pl.program_id(0)

    @pl.when(o == 0)
    def _():
        for n in range(REACH):
            keys[n * tok : (n + 1) * tok] = before[n, 0]
            values[n * tok : (n + 1) * tok] = before[n, 1]
        for n in range(KVH):
            at = slice((REACH + n) * tok, (REACH + n + 1) * tok)
            keys[at] = row[n, 0]
            values[at] = row[n, 1]
        gk[...] = jnp.zeros_like(gk)
        gv[...] = jnp.zeros_like(gv)

    for n, block in enumerate((q0, q1, q2, q3)):

        @pl.when(o == n)
        def _(block=block):
            qd[...] = block[...]

    run = (where[1] + KVH - o) & (KVH - 1)
    start = (where[0] * KVH + run) * tok
    qpos = start + lax.broadcasted_iota(jnp.int32, (8, tok), 1)

    def step(n, carry):
        end, first = carry
        end = end + lens[n]
        return end, jnp.where(end <= qpos, end, first)

    _, first = lax.fori_loop(
        0, lens.shape[0], step, (jnp.int32(0), jnp.zeros((8, tok), jnp.int32))
    )
    kpos = start - REACH * tok + lax.broadcasted_iota(jnp.int32, (win, tok), 0)
    ok = (kpos >= first[0:1]) & (kpos <= qpos[0:1])
    bias[...] = jnp.where(ok, 0.0, -1e30).astype(F32)

    here = pl.ds(pl.multiple_of(run * tok, tok), win)
    k = keys[here, :]
    v = values[here, :]
    for r in range(GROUP):
        at = slice(r * HD, (r + 1) * HD)
        rows = slice(r * tok, (r + 1) * tok)
        s = dot(k, qd[0, :, at], 1, 1) * (SCALE * LOG2E) + bias[...]
        dp = dot(v, qd[1, :, at], 1, 1)
        e = jnp.exp2(s - jnp.max(s, axis=0, keepdims=True))
        p = e * (1.0 / jnp.sum(e, axis=0, keepdims=True))
        delta = jnp.sum(p * dp, axis=0, keepdims=True)
        probs[:, rows] = p.astype(BF16)
        dscores[:, rows] = (p * (dp - delta)).astype(BF16)
    qs = jnp.concatenate([qd[0, :, r * HD : (r + 1) * HD] for r in range(GROUP)], axis=0)
    dos = jnp.concatenate([qd[1, :, r * HD : (r + 1) * HD] for r in range(GROUP)], axis=0)
    gk[here, :] = gk[here, :] + dot(dscores[...], qs, 1, 0) * SCALE
    gv[here, :] = gv[here, :] + dot(probs[...], dos, 1, 0)

    @pl.when(o == KVH - 1)
    def _():
        for n in range(REACH):
            back[n, 0] = gk[n * tok : (n + 1) * tok].astype(BF16)
            back[n, 1] = gv[n * tok : (n + 1) * tok].astype(BF16)
        for n in range(KVH):
            at = slice((REACH + n) * tok, (REACH + n + 1) * tok)
            own[n, 0] = gk[at]
            own[n, 1] = gv[at]


def attend(where, lens, qs, row, before):
    tok = row.shape[2]
    win, span = (REACH + 1) * tok, (REACH + KVH) * tok
    wide = GROUP * HD

    def whole(*shape):
        return pl.BlockSpec(shape, lambda o: (0,) * len(shape))

    return pl.pallas_call(
        attend_kernel,
        grid=(KVH,),
        in_specs=[SMEM, SMEM]
        + [whole(2, tok, wide)] * KVH
        + [whole(KVH, 2, tok, HD), whole(REACH, 2, tok, HD)],
        out_specs=[whole(REACH, 2, tok, HD), whole(KVH, 2, tok, HD)],
        out_shape=[
            jax.ShapeDtypeStruct((REACH, 2, tok, HD), BF16),
            jax.ShapeDtypeStruct((KVH, 2, tok, HD), F32),
        ],
        scratch_shapes=[
            pltpu.VMEM((2, tok, wide), BF16),
            pltpu.VMEM((span, HD), BF16),
            pltpu.VMEM((span, HD), BF16),
            pltpu.VMEM((span, HD), F32),
            pltpu.VMEM((span, HD), F32),
            pltpu.VMEM((win, tok), F32),
            pltpu.VMEM((win, GROUP * tok), BF16),
            pltpu.VMEM((win, GROUP * tok), BF16),
        ],
        compiler_params=params(40),
    )(where, lens, *qs, row, before)


def mixing_line(part, grads):
    sums = []
    for i in range(NPHM):
        for a in range(NPHM):
            for b in range(NPHM):
                both = part[a, :, i * HD : (i + 1) * HD] * grads[:, b * HD : (b + 1) * HD]
                sums.append(jnp.sum(both, axis=0, keepdims=True))
    sums = jnp.sum(jnp.concatenate(sums, axis=0), axis=1, keepdims=True)
    many = NPHM**3
    spot = lax.broadcasted_iota(jnp.int32, (many, HD), 0)
    lane = lax.broadcasted_iota(jnp.int32, (many, HD), 1)
    return jnp.sum(jnp.where(spot == lane, sums, 0.0), axis=0, keepdims=True)


def factor_kernel(which, mix, *refs):
    xs, (gm, go), refs = refs[:8], refs[8:10], refs[10:]
    (mixed, grads), refs = refs[-2:], refs[:-2]
    j = pl.program_id(0)
    tok = gm.shape[1]

    @pl.when(j == 0)
    def _():
        for b in range(NPHM):
            grads[:tok, b * HD : (b + 1) * HD] = gm[b].astype(F32)
            grads[tok:, b * HD : (b + 1) * HD] = go[b].astype(F32)
        for a in range(NPHM):
            for n, i in enumerate(which):
                total = mix[i * 16 + a * 4] * grads[:, :HD]
                for b in range(1, NPHM):
                    total = total + mix[i * 16 + a * 4 + b] * grads[:, b * HD : (b + 1) * HD]
                mixed[a, :, n * HD : (n + 1) * HD] = total.astype(BF16)
        if 0 in which:
            row = refs[-1]
            row[...] = jnp.broadcast_to(mixing_line(refs[0], grads), row.shape)

    total = None
    for a in range(NPHM):
        x = jnp.concatenate([xs[a][0], xs[4 + a][0]], axis=0)
        one = dot(mixed[a], x, 0, 0)
        total = one if total is None else total + one
    outs = refs[1:3] if 0 in which else refs[:2]
    for n, out in enumerate(outs):
        out[...] = total[n * HD : (n + 1) * HD].astype(BF16)


def factor_grads(which, mix, xm, xo, gm, go, part=None):
    tok, width = xm.shape[1:]
    dq, cols = width // NPHM, NPHM * HD
    steps = 4
    wide = dq // steps
    xspecs = [
        pl.BlockSpec((1, tok, wide), functools.partial(lambda a, j: (0, 0, a * steps + j), a))
        for a in range(NPHM)
    ]
    whole = pl.BlockSpec((NPHM, tok, HD), lambda j: (0, 0, 0))
    ins = [SMEM] + xspecs + xspecs + [whole, whole]
    args = [mix] + [xm] * 4 + [xo] * 4 + [gm, go]
    out_specs = [pl.BlockSpec((HD, wide), lambda j: (0, j))] * 2
    out_shape = [jax.ShapeDtypeStruct((HD, dq), BF16)] * 2
    if part is not None:
        ins.append(pl.BlockSpec((NPHM, 2 * tok, cols), lambda j: (0, 0, 0)))
        args.append(part)
        out_specs.append(pl.BlockSpec((8, HD), lambda j: (0, 0)))
        out_shape.append(jax.ShapeDtypeStruct((8, HD), F32))
    return pl.pallas_call(
        functools.partial(factor_kernel, which),
        grid=(steps,),
        in_specs=ins,
        out_specs=out_specs,
        out_shape=out_shape,
        scratch_shapes=[
            pltpu.VMEM((NPHM, 2 * tok, 2 * HD), BF16),
            pltpu.VMEM((2 * tok, cols), F32),
        ],
        compiler_params=params(40),
    )(*args)


def split_line(value):
    lane = lax.broadcasted_iota(jnp.int32, value.shape, 1)
    high = value.astype(BF16).astype(F32)
    return jnp.where(lane < HD // 2, high, value - high)


def turn_kernel(t0, t1, t2, t3, row, out):
    n, rows = out.shape[0], out.shape[1] - PAD
    total = t0[...].astype(F32)
    for t in (t1, t2, t3):
        total = total + t[...].astype(F32)
    turned = total.T.astype(BF16)
    line = row[0:1]
    line = line + jnp.concatenate([line[:, HD // 2 :], line[:, : HD // 2]], axis=1)
    line = jnp.broadcast_to(split_line(line), (PAD, HD)).astype(BF16)
    for d in range(n):
        out[d, :rows] = turned[d * rows : (d + 1) * rows]
        out[d, rows:] = line


def turn(terms, row, n):
    rows = terms[0].shape[1] // n
    return pl.pallas_call(
        turn_kernel,
        out_shape=jax.ShapeDtypeStruct((n, rows + PAD, HD), BF16),
        compiler_params=params(40),
    )(*terms, row)


def total_kernel(blocks, out):
    rows = out.shape[1] - PAD
    total = blocks[0].astype(F32)
    for d in range(1, blocks.shape[0]):
        total = total + blocks[d].astype(F32)
    line = total[rows : rows + 1]
    line = line + jnp.concatenate([line[:, HD // 2 :], line[:, : HD // 2]], axis=1)
    line = jnp.broadcast_to(split_line(line), (PAD, HD)).astype(BF16)
    body = total[:rows].astype(BF16)
    for d in range(out.shape[0]):
        out[d, :rows] = body
        out[d, rows:] = line


def total(blocks, n):
    return pl.pallas_call(
        total_kernel,
        out_shape=jax.ShapeDtypeStruct((n,) + blocks.shape[1:], BF16),
        compiler_params=params(40),
    )(blocks)


def final_kernel(blocks, gk, gv, mk, mv):
    half = NPHM * 2
    rows = gk.shape[0]
    lines = [None, None]
    for i in range(NPHM):
        for c, out in enumerate((gk, gv)):
            at = i * 2 + c
            block = blocks[at].astype(F32)
            for z in range(at + half, blocks.shape[0], half):
                block = block + blocks[z].astype(F32)
            out[:, i, :] = block[:rows]
            line = block[rows : rows + 1]
            lines[c] = line if lines[c] is None else lines[c] + line
    row = lax.broadcasted_iota(jnp.int32, (NPHM, HD), 0)
    lane = lax.broadcasted_iota(jnp.int32, (NPHM, HD), 1)
    col = lax.broadcasted_iota(jnp.int32, (NPHM, NPHM), 1)
    for line, out in zip(lines, (mk, mv)):
        for i in range(NPHM):
            tile = jnp.zeros((NPHM, NPHM), F32)
            for b in range(NPHM):
                mine = (lane & (HD // 2 - 1)) == i * 16 + row * 4 + b
                tile = jnp.where(col == b, jnp.sum(jnp.where(mine, line, 0.0), axis=1, keepdims=True), tile)
            out[i] = tile


def final(blocks, rows):
    return pl.pallas_call(
        final_kernel,
        out_shape=[jax.ShapeDtypeStruct((rows, NPHM, HD), F32)] * 2
        + [jax.ShapeDtypeStruct((NPHM, NPHM, NPHM), F32)] * 2,
        compiler_params=params(40),
    )(blocks)


def shards(inputs, queries, upstream, lengths, factor_k, factor_v, mixing_k, mixing_v):
    tok = inputs.shape[1]
    rows = factor_k.shape[0]
    n_ctx = lax.axis_size("y") * lax.axis_size("zl")
    n_dp = lax.axis_size("zh") * lax.axis_size("x") * lax.axis_size("c")
    z_at = lax.axis_index("zl")
    x_at = lax.axis_index("x")
    first = lax.axis_index("c") == 0
    swap = [(0, 1), (1, 0)]

    other = lax.ppermute(inputs, "c", swap)
    mix = jnp.where(first, mixing_k, mixing_v)
    turned = lax.dynamic_slice_in_dim(jnp.concatenate([mix, mix]), x_at, NPHM, 0).reshape(-1)
    mine = lax.dynamic_index_in_dim(
        jnp.where(first, factor_k, factor_v), x_at, axis=1, keepdims=False
    )
    piece = jnp.broadcast_to(mine[None], (n_ctx, rows, HD))
    wide = GROUP * HD
    blocks = []
    for o in range(KVH):
        head = ((z_at + o) & (KVH - 1)) * wide
        blocks.append(
            jnp.stack([lax.dynamic_slice_in_dim(m[0], head, wide, 1) for m in (queries, upstream)])
        )
    piece = lax.all_to_all(piece, CTX, 0, 0, tiled=True).reshape(1, n_ctx * rows, HD)
    q1 = lax.ppermute(blocks[1], "zl", around(1))
    piece, q1, b2 = lax.optimization_barrier((piece, q1, blocks[2]))
    q2 = lax.ppermute(b2, "zl", around(2))
    weights = lax.all_to_all(
        jnp.broadcast_to(piece, (NPHM, n_ctx * rows, HD)), "x", 0, 0, tiled=True
    )
    weights, q2, b3 = lax.optimization_barrier((weights, q2, blocks[3]))
    q3 = lax.ppermute(b3, "zl", around(3))
    part, both = project(mix.reshape(-1), inputs, other, weights)

    got = lax.ppermute(both[1], "c", swap)
    pack = jnp.stack([jnp.where(first, both[0], got), jnp.where(first, got, both[0])], axis=1)
    pack, q3 = lax.optimization_barrier((pack, q3))
    row = lax.all_to_all(pack, "zl", 0, 0, tiled=True)
    up = [(n, n + 1) for n in range(lax.axis_size("y") - 1)]
    before = lax.ppermute(row[KVH - REACH :], "y", up)
    where = jnp.stack([lax.axis_index("y"), z_at]).astype(jnp.int32)
    back, own = attend(where, lengths[0], [blocks[0], q1, q2, q3], row, before)
    back = lax.ppermute(back, "y", [(n, m) for m, n in up]).astype(F32)
    own = jnp.concatenate([own[: KVH - REACH], own[KVH - REACH :] + back])
    grads = lax.all_to_all(own.astype(BF16), "zl", 0, 0, tiled=True)
    keep = jnp.where(first, grads[:, 0], grads[:, 1])
    got = lax.ppermute(jnp.where(first, grads[:, 1], grads[:, 0]), "c", swap)

    one, three = factor_grads((1, 3), turned, inputs, other, keep, got)
    sent = [lax.ppermute(one, "x", around(1)), lax.ppermute(three, "x", around(3))]
    own, two, row = factor_grads((0, 2), turned, inputs, other, keep, got, part)
    sent.append(lax.ppermute(two, "x", around(2)))
    blocks = lax.all_to_all(turn([own] + sent, row, n_ctx), CTX, 0, 0, tiled=True)
    blocks = lax.all_to_all(total(blocks, n_dp), DP, 0, 0, tiled=True)
    return tuple(final(blocks, rows))


def solution(mesh):
    n_dp, n_ctx = mesh.devices.shape
    zl = 4
    shape = (n_dp // 8, 4, 2, n_ctx // zl, zl)
    wide = Mesh(mesh.devices.reshape(shape), DP + CTX)
    in_specs = (
        P(DP, CTX, None),
        P(DP, CTX, None),
        P(DP, CTX, None),
        P(DP, None),
        P(CTX, None, None),
        P(CTX, None, None),
        P(),
        P(),
    )
    out_specs = (P(CTX, None, None), P(CTX, None, None), P(), P())
    return jax.shard_map(shards, mesh=wide, in_specs=in_specs, out_specs=out_specs, check_vma=False)
```

```python
import functools
import math

import jax
import jax.numpy as jnp
from jax import lax
from jax.experimental import pallas as pl
from jax.experimental.pallas import tpu as pltpu
from jax.sharding import Mesh, PartitionSpec as P

KVH = 4
HD = 128
REACH = 3
GROUP = 8
NPHM = 4
PAD = 16
CTX = ("y", "zl")
DP = ("zh", "x", "c")
SCALE = 1.0 / math.sqrt(HD)
LOG2E = 1.4426950408889634
SMEM = pl.BlockSpec(memory_space=pltpu.SMEM)
F32 = jnp.float32
BF16 = jnp.bfloat16


def dot(a, b, ca, cb):
    return lax.dot_general(a, b, (((ca,), (cb,)), ((), ())), preferred_element_type=F32)


def around(distance):
    return [(i, (i + distance) % NPHM) for i in range(NPHM)]


def params(mib):
    return pltpu.CompilerParams(vmem_limit_bytes=mib << 20)


def chunks(x, steps):
    tok, width = x.shape[1:]
    wide = width // NPHM // steps
    return [
        pl.BlockSpec((1, tok, wide), functools.partial(lambda a, j: (0, 0, a * steps + j), a))
        for a in range(NPHM)
    ]


def stacked(xs):
    return jnp.concatenate([xs[n * NPHM + a][0] for a in range(NPHM) for n in range(2)], axis=0)


def project_kernel(mix, core, *refs):
    xs, (w, part, out) = refs[:8], refs[8:]
    j = pl.program_id(0)
    tok = xs[0].shape[1]
    one = dot(stacked(xs), jnp.concatenate([w[i] for i in range(NPHM)], axis=1), 1, 0)

    @pl.when(j == 0)
    def _():
        for a in range(NPHM):
            part[a] = one[2 * a * tok : 2 * (a + 1) * tok]

    @pl.when(j > 0)
    def _():
        for a in range(NPHM):
            part[a] = part[a] + one[2 * a * tok : 2 * (a + 1) * tok]

    @pl.when(j == pl.num_programs(0) - 1)
    def _():
        for b in range(NPHM):
            total = None
            for a in range(NPHM):
                for i in range(NPHM):
                    term = mix[i * 16 + a * 4 + b] * part[a, :, i * HD : (i + 1) * HD]
                    total = term if total is None else total + term
            total = total.astype(BF16)
            out[core[0], b] = total[:tok]
            out[1 - core[0], b] = total[tok:]


def project(mix, core, xm, xo, w):
    tok, width = xm.shape[1:]
    dq, cols = width // NPHM, NPHM * HD
    steps = 4
    return pl.pallas_call(
        project_kernel,
        grid=(steps,),
        in_specs=[SMEM, SMEM]
        + chunks(xm, steps)
        + chunks(xo, steps)
        + [pl.BlockSpec((NPHM, dq // steps, HD), lambda j: (0, j, 0))],
        out_specs=[
            pl.BlockSpec((NPHM, 2 * tok, cols), lambda j: (0, 0, 0)),
            pl.BlockSpec((2, NPHM, tok, HD), lambda j: (0, 0, 0, 0)),
        ],
        out_shape=[
            jax.ShapeDtypeStruct((NPHM, 2 * tok, cols), F32),
            jax.ShapeDtypeStruct((2, NPHM, tok, HD), BF16),
        ],
        compiler_params=params(32),
    )(mix, core, *([xm] * 4), *([xo] * 4), w)


def attend_kernel(
    where, lens, q0, q1, q2, q3, row, before, back, own, *scratch
):
    q, do, keys, values, gk, gv, bias, probs, dscores = scratch
    tok = q0.shape[1]
    win = (REACH + 1) * tok
    o = pl.program_id(0)

    @pl.when(o == 0)
    def _():
        for n in range(REACH):
            keys[n * tok : (n + 1) * tok] = before[0, n]
            values[n * tok : (n + 1) * tok] = before[1, n]
        for n in range(KVH):
            at = slice((REACH + n) * tok, (REACH + n + 1) * tok)
            keys[at] = row[0, n]
            values[at] = row[1, n]
        gk[...] = jnp.zeros_like(gk)
        gv[...] = jnp.zeros_like(gv)

    for n, block in enumerate((q0, q1, q2, q3)):

        @pl.when(o == n)
        def _(block=block):
            for r in range(GROUP):
                q[r * tok : (r + 1) * tok] = block[0, :, r * HD : (r + 1) * HD]
                do[r * tok : (r + 1) * tok] = block[1, :, r * HD : (r + 1) * HD]

    run = (where[1] + KVH - o) & (KVH - 1)
    start = (where[0] * KVH + run) * tok
    qpos = start + lax.broadcasted_iota(jnp.int32, (8, tok), 1)

    def step(n, carry):
        end, first = carry
        end = end + lens[n]
        return end, jnp.where(end <= qpos, end, first)

    _, first = lax.fori_loop(
        0, lens.shape[0], step, (jnp.int32(0), jnp.zeros((8, tok), jnp.int32))
    )
    kpos = start - REACH * tok + lax.broadcasted_iota(jnp.int32, (win, tok), 0)
    ok = (kpos >= first[0:1]) & (kpos <= qpos[0:1])
    once = jnp.where(ok, 0.0, -1e30).astype(F32)
    bias[:, :tok] = once
    bias[:, tok:] = once

    here = pl.ds(pl.multiple_of(run * tok, tok), win)
    k = keys[here, :]
    v = values[here, :]
    for r in range(0, GROUP, 2):
        rows = slice(r * tok, (r + 2) * tok)
        s = dot(k, q[rows], 1, 1) * (SCALE * LOG2E) + bias[...]
        dp = dot(v, do[rows], 1, 1)
        e = jnp.exp2(s - jnp.max(s, axis=0, keepdims=True))
        p = e * (1.0 / jnp.sum(e, axis=0, keepdims=True))
        delta = jnp.sum(p * dp, axis=0, keepdims=True)
        probs[:, rows] = p.astype(BF16)
        dscores[:, rows] = (p * (dp - delta)).astype(BF16)
    gk[here, :] = gk[here, :] + dot(dscores[...], q[...], 1, 0) * SCALE
    gv[here, :] = gv[here, :] + dot(probs[...], do[...], 1, 0)

    @pl.when(o == KVH - 1)
    def _():
        for n in range(REACH):
            back[0, n] = gk[n * tok : (n + 1) * tok].astype(BF16)
            back[1, n] = gv[n * tok : (n + 1) * tok].astype(BF16)
        for n in range(KVH):
            at = slice((REACH + n) * tok, (REACH + n + 1) * tok)
            own[0, n] = gk[at]
            own[1, n] = gv[at]


def attend(where, lens, qs, row, before):
    tok = row.shape[2]
    win, span = (REACH + 1) * tok, (REACH + KVH) * tok
    wide = GROUP * HD

    def whole(*shape):
        return pl.BlockSpec(shape, lambda o: (0,) * len(shape))

    return pl.pallas_call(
        attend_kernel,
        grid=(KVH,),
        in_specs=[SMEM, SMEM]
        + [whole(2, tok, wide)] * KVH
        + [whole(2, KVH, tok, HD), whole(2, REACH, tok, HD)],
        out_specs=[whole(2, REACH, tok, HD), whole(2, KVH, tok, HD)],
        out_shape=[
            jax.ShapeDtypeStruct((2, REACH, tok, HD), BF16),
            jax.ShapeDtypeStruct((2, KVH, tok, HD), F32),
        ],
        scratch_shapes=[
            pltpu.VMEM((GROUP * tok, HD), BF16),
            pltpu.VMEM((GROUP * tok, HD), BF16),
            pltpu.VMEM((span, HD), BF16),
            pltpu.VMEM((span, HD), BF16),
            pltpu.VMEM((span, HD), F32),
            pltpu.VMEM((span, HD), F32),
            pltpu.VMEM((win, 2 * tok), F32),
            pltpu.VMEM((win, GROUP * tok), BF16),
            pltpu.VMEM((win, GROUP * tok), BF16),
        ],
        compiler_params=params(24),
    )(where, lens, *qs, row, before)


def mixing_line(part, grads):
    sums = []
    for i in range(NPHM):
        for a in range(NPHM):
            for b in range(NPHM):
                both = part[a, :, i * HD : (i + 1) * HD] * grads[:, b * HD : (b + 1) * HD]
                sums.append(jnp.sum(both, axis=0, keepdims=True))
    sums = jnp.sum(jnp.concatenate(sums, axis=0), axis=1, keepdims=True)
    many = NPHM**3
    spot = lax.broadcasted_iota(jnp.int32, (many, HD), 0)
    lane = lax.broadcasted_iota(jnp.int32, (many, HD), 1)
    return jnp.sum(jnp.where(spot == lane, sums, 0.0), axis=0, keepdims=True)


def factor_kernel(which, mix, core, *refs):
    xs, g, refs = refs[:8], refs[8], refs[9:]
    (mixed, grads), refs = refs[-2:], refs[:-2]
    tok = g.shape[2]

    @pl.when(pl.program_id(0) == 0)
    def _():
        for b in range(NPHM):
            grads[:tok, b * HD : (b + 1) * HD] = g[core[0], b].astype(F32)
            grads[tok:, b * HD : (b + 1) * HD] = g[1 - core[0], b].astype(F32)
        for a in range(NPHM):
            for n, i in enumerate(which):
                total = mix[i * 16 + a * 4] * grads[:, :HD]
                for b in range(1, NPHM):
                    total = total + mix[i * 16 + a * 4 + b] * grads[:, b * HD : (b + 1) * HD]
                mixed[n * HD : (n + 1) * HD, 2 * a * tok : 2 * (a + 1) * tok] = total.T.astype(BF16)
        if 0 in which:
            line = mixing_line(refs[0], grads)
            line = line + jnp.concatenate([line[:, HD // 2 :], line[:, : HD // 2]], axis=1)
            line = jnp.broadcast_to(split_line(line), (PAD, HD)).astype(BF16)
            for d in range(refs[-1].shape[0]):
                refs[-1][d] = line

    total = dot(mixed[...], stacked(xs), 1, 0)
    outs = refs[1:3] if 0 in which else refs[:2]
    for n, out in enumerate(outs):
        out[...] = total[n * HD : (n + 1) * HD].astype(BF16)


def factor_grads(which, mix, core, xm, xo, g, part=None, n=0):
    tok, width = xm.shape[1:]
    dq, cols = width // NPHM, NPHM * HD
    steps = 4
    ins = [SMEM, SMEM] + chunks(xm, steps) + chunks(xo, steps)
    ins.append(pl.BlockSpec((2, NPHM, tok, HD), lambda j: (0, 0, 0, 0)))
    args = [mix, core] + [xm] * 4 + [xo] * 4 + [g]
    out_specs = [pl.BlockSpec((HD, dq // steps), lambda j: (0, j))] * 2
    out_shape = [jax.ShapeDtypeStruct((HD, dq), BF16)] * 2
    if part is not None:
        ins.append(pl.BlockSpec((NPHM, 2 * tok, cols), lambda j: (0, 0, 0)))
        args.append(part)
        out_specs.append(pl.BlockSpec((n, PAD, HD), lambda j: (0, 0, 0)))
        out_shape.append(jax.ShapeDtypeStruct((n, PAD, HD), BF16))
    return pl.pallas_call(
        functools.partial(factor_kernel, which),
        grid=(steps,),
        in_specs=ins,
        out_specs=out_specs,
        out_shape=out_shape,
        scratch_shapes=[
            pltpu.VMEM((2 * HD, NPHM * 2 * tok), BF16),
            pltpu.VMEM((2 * tok, cols), F32),
        ],
        compiler_params=params(32),
    )(*args)


def split_line(value):
    lane = lax.broadcasted_iota(jnp.int32, value.shape, 1)
    high = value.astype(BF16).astype(F32)
    return jnp.where(lane < HD // 2, high, value - high)


def turn_kernel(t0, t1, t2, t3, out):
    n, rows = out.shape[:2]
    total = t0[...].astype(F32)
    for t in (t1, t2, t3):
        total = total + t[...].astype(F32)
    turned = total.T.astype(BF16)
    for d in range(n):
        out[d] = turned[d * rows : (d + 1) * rows]


def turn(terms, n):
    rows = terms[0].shape[1] // n
    return pl.pallas_call(
        turn_kernel,
        out_shape=jax.ShapeDtypeStruct((n, rows, HD), BF16),
        compiler_params=params(40),
    )(*terms)


def total_kernel(blocks, lines, out):
    rows = blocks.shape[1]
    total, line = blocks[0].astype(F32), lines[0].astype(F32)
    for d in range(1, blocks.shape[0]):
        total = total + blocks[d].astype(F32)
        line = line + lines[d].astype(F32)
    line = line + jnp.concatenate([line[:, HD // 2 :], line[:, : HD // 2]], axis=1)
    line = split_line(line).astype(BF16)
    body = total.astype(BF16)
    for d in range(out.shape[0]):
        out[d, :rows] = body
        out[d, rows:] = line


def total(blocks, lines, n):
    rows = blocks.shape[1] + PAD
    return pl.pallas_call(
        total_kernel,
        out_shape=jax.ShapeDtypeStruct((n, rows, HD), BF16),
        compiler_params=params(40),
    )(blocks, lines)


def final_kernel(blocks, gk, gv, mk, mv):
    half = NPHM * 2
    rows = gk.shape[0]
    lines = [None, None]
    for i in range(NPHM):
        for c, out in enumerate((gk, gv)):
            at = i * 2 + c
            block = blocks[at].astype(F32)
            for z in range(at + half, blocks.shape[0], half):
                block = block + blocks[z].astype(F32)
            out[:, i, :] = block[:rows]
            line = block[rows : rows + 1]
            lines[c] = line if lines[c] is None else lines[c] + line
    row = lax.broadcasted_iota(jnp.int32, (NPHM, HD), 0)
    lane = lax.broadcasted_iota(jnp.int32, (NPHM, HD), 1)
    col = lax.broadcasted_iota(jnp.int32, (NPHM, NPHM), 1)
    for line, out in zip(lines, (mk, mv)):
        for i in range(NPHM):
            tile = jnp.zeros((NPHM, NPHM), F32)
            for b in range(NPHM):
                mine = (lane & (HD // 2 - 1)) == i * 16 + row * 4 + b
                tile = jnp.where(col == b, jnp.sum(jnp.where(mine, line, 0.0), axis=1, keepdims=True), tile)
            out[i] = tile


def final(blocks, rows):
    return pl.pallas_call(
        final_kernel,
        out_shape=[jax.ShapeDtypeStruct((rows, NPHM, HD), F32)] * 2
        + [jax.ShapeDtypeStruct((NPHM, NPHM, NPHM), F32)] * 2,
        compiler_params=params(40),
    )(blocks)


def shards(inputs, queries, upstream, lengths, factor_k, factor_v, mixing_k, mixing_v):
    tok = inputs.shape[1]
    rows = factor_k.shape[0]
    n_ctx = lax.axis_size("y") * lax.axis_size("zl")
    n_dp = lax.axis_size("zh") * lax.axis_size("x") * lax.axis_size("c")
    z_at = lax.axis_index("zl")
    x_at = lax.axis_index("x")
    first = lax.axis_index("c") == 0
    swap = [(0, 1), (1, 0)]

    other = lax.ppermute(inputs, "c", swap)
    mix = jnp.where(first, mixing_k, mixing_v)
    turned = lax.dynamic_slice_in_dim(jnp.concatenate([mix, mix]), x_at, NPHM, 0).reshape(-1)
    mine = lax.dynamic_index_in_dim(
        jnp.where(first, factor_k, factor_v), x_at, axis=1, keepdims=False
    )
    n_y, n_z = lax.axis_size("y"), lax.axis_size("zl")
    core = lax.axis_index("c").astype(jnp.int32).reshape(1)
    piece = jnp.broadcast_to(mine[None], (n_z, rows, HD))
    wide = GROUP * HD
    blocks = []
    for o in range(KVH):
        head = ((z_at + o) & (KVH - 1)) * wide
        blocks.append(
            jnp.stack([lax.dynamic_slice_in_dim(m[0], head, wide, 1) for m in (queries, upstream)])
        )
    piece = lax.all_to_all(piece, "zl", 0, 0, tiled=True).reshape(1, n_z * rows, HD)
    piece = lax.all_to_all(
        jnp.broadcast_to(piece, (n_y, n_z * rows, HD)), "y", 0, 0, tiled=True
    ).reshape(1, n_ctx * rows, HD)
    q1 = lax.ppermute(blocks[1], "zl", around(1))
    piece, q1, b2 = lax.optimization_barrier((piece, q1, blocks[2]))
    q2 = lax.ppermute(b2, "zl", around(2))
    weights = lax.all_to_all(
        jnp.broadcast_to(piece, (NPHM, n_ctx * rows, HD)), "x", 0, 0, tiled=True
    )
    weights, q2, b3 = lax.optimization_barrier((weights, q2, blocks[3]))
    q3 = lax.ppermute(b3, "zl", around(3))
    part, both = project(mix.reshape(-1), core, inputs, other, weights)

    both, q3 = lax.optimization_barrier((both, q3))
    row = lax.all_to_all(both.reshape(2 * KVH, tok, HD), ("c", "zl"), 0, 0, tiled=True)
    row = row.reshape(2, KVH, tok, HD)
    up = [(n, n + 1) for n in range(lax.axis_size("y") - 1)]
    before = lax.ppermute(row[:, KVH - REACH :], "y", up)
    where = jnp.stack([lax.axis_index("y"), z_at]).astype(jnp.int32)
    back, own = attend(where, lengths[0], [blocks[0], q1, q2, q3], row, before)
    back = lax.ppermute(back, "y", [(n, m) for m, n in up]).astype(F32)
    own = own + jnp.pad(back, ((0, 0), (KVH - REACH, 0), (0, 0), (0, 0)))
    grads = own.astype(BF16).reshape(2 * KVH, tok, HD)
    grads = lax.all_to_all(grads, ("c", "zl"), 0, 0, tiled=True).reshape(2, KVH, tok, HD)

    one, three = factor_grads((1, 3), turned, core, inputs, other, grads)
    sent = [lax.ppermute(one, "x", around(1)), lax.ppermute(three, "x", around(3))]
    own, two, lines = factor_grads((0, 2), turned, core, inputs, other, grads, part, n_ctx)
    sent.append(lax.ppermute(two, "x", around(2)))
    lines = lax.all_to_all(lines, CTX, 0, 0, tiled=True)
    blocks = lax.all_to_all(turn([own] + sent, n_ctx), CTX, 0, 0, tiled=True)
    blocks = lax.all_to_all(total(blocks, lines, n_dp), DP, 0, 0, tiled=True)
    return tuple(final(blocks, rows))


def solution(mesh):
    n_dp, n_ctx = mesh.devices.shape
    zl = 4
    shape = (n_dp // 8, 4, 2, n_ctx // zl, zl)
    wide = Mesh(mesh.devices.reshape(shape), DP + CTX)
    in_specs = (
        P(DP, CTX, None),
        P(DP, CTX, None),
        P(DP, CTX, None),
        P(DP, None),
        P(CTX, None, None),
        P(CTX, None, None),
        P(),
        P(),
    )
    out_specs = (P(CTX, None, None), P(CTX, None, None), P(), P())
    return jax.shard_map(shards, mesh=wide, in_specs=in_specs, out_specs=out_specs, check_vma=False)
```

```python
import functools
import math

import jax
import jax.numpy as jnp
from jax import lax
from jax.experimental import pallas as pl
from jax.experimental.pallas import tpu as pltpu
from jax.sharding import Mesh, PartitionSpec as P

KVH = 4
HD = 128
REACH = 3
GROUP = 8
NPHM = 4
PAD = 16
CTX = ("y", "zl")
DP = ("zh", "x", "c")
SCALE = 1.0 / math.sqrt(HD)
LOG2E = 1.4426950408889634
SMEM = pl.BlockSpec(memory_space=pltpu.SMEM)
F32 = jnp.float32
BF16 = jnp.bfloat16


def dot(a, b, ca, cb):
    return lax.dot_general(a, b, (((ca,), (cb,)), ((), ())), preferred_element_type=F32)


def around(distance):
    return [(i, (i + distance) % NPHM) for i in range(NPHM)]


def params(mib):
    return pltpu.CompilerParams(vmem_limit_bytes=mib << 20)


def chunks(x, steps):
    tok, width = x.shape[1:]
    wide = width // NPHM // steps
    return [
        pl.BlockSpec((1, tok, wide), functools.partial(lambda a, j: (0, 0, a * steps + j), a))
        for a in range(NPHM)
    ]


def stacked(xs):
    return jnp.concatenate([xs[n * NPHM + a][0] for a in range(NPHM) for n in range(2)], axis=0)


def project_kernel(mix, core, *refs):
    xs, (w, part, out) = refs[:8], refs[8:]
    j = pl.program_id(0)
    tok = xs[0].shape[1]
    one = dot(stacked(xs), jnp.concatenate([w[i] for i in range(NPHM)], axis=1), 1, 0)

    @pl.when(j == 0)
    def _():
        for a in range(NPHM):
            part[a] = one[2 * a * tok : 2 * (a + 1) * tok]

    @pl.when(j > 0)
    def _():
        for a in range(NPHM):
            part[a] = part[a] + one[2 * a * tok : 2 * (a + 1) * tok]

    @pl.when(j == pl.num_programs(0) - 1)
    def _():
        for b in range(NPHM):
            total = None
            for a in range(NPHM):
                for i in range(NPHM):
                    term = mix[i * 16 + a * 4 + b] * part[a, :, i * HD : (i + 1) * HD]
                    total = term if total is None else total + term
            total = total.astype(BF16)
            out[core[0], b] = total[:tok]
            out[1 - core[0], b] = total[tok:]


def project(mix, core, xm, xo, w):
    tok, width = xm.shape[1:]
    dq, cols = width // NPHM, NPHM * HD
    steps = 4
    return pl.pallas_call(
        project_kernel,
        grid=(steps,),
        in_specs=[SMEM, SMEM]
        + chunks(xm, steps)
        + chunks(xo, steps)
        + [pl.BlockSpec((NPHM, dq // steps, HD), lambda j: (0, j, 0))],
        out_specs=[
            pl.BlockSpec((NPHM, 2 * tok, cols), lambda j: (0, 0, 0)),
            pl.BlockSpec((2, NPHM, tok, HD), lambda j: (0, 0, 0, 0)),
        ],
        out_shape=[
            jax.ShapeDtypeStruct((NPHM, 2 * tok, cols), F32),
            jax.ShapeDtypeStruct((2, NPHM, tok, HD), BF16),
        ],
        compiler_params=params(32),
    )(mix, core, *([xm] * 4), *([xo] * 4), w)


def attend_kernel(
    where, lens, q0, q1, q2, q3, row, before, back, own, *scratch
):
    q, do, keys, values, gk, gv, bias, probs, dscores = scratch
    tok = q0.shape[1]
    win = (REACH + 1) * tok
    o = pl.program_id(0)

    @pl.when(o == 0)
    def _():
        for n in range(REACH):
            keys[n * tok : (n + 1) * tok] = before[0, n]
            values[n * tok : (n + 1) * tok] = before[1, n]
        for n in range(KVH):
            at = slice((REACH + n) * tok, (REACH + n + 1) * tok)
            keys[at] = row[0, n]
            values[at] = row[1, n]
        gk[...] = jnp.zeros_like(gk)
        gv[...] = jnp.zeros_like(gv)

    for n, block in enumerate((q0, q1, q2, q3)):

        @pl.when(o == n)
        def _(block=block):
            for r in range(GROUP):
                q[r * tok : (r + 1) * tok] = block[0, :, r * HD : (r + 1) * HD]
                do[r * tok : (r + 1) * tok] = block[1, :, r * HD : (r + 1) * HD]

    run = (where[1] + KVH - o) & (KVH - 1)
    start = (where[0] * KVH + run) * tok
    qpos = start + lax.broadcasted_iota(jnp.int32, (8, tok), 1)

    def step(n, carry):
        end, first = carry
        end = end + lens[n]
        return end, jnp.where(end <= qpos, end, first)

    _, first = lax.fori_loop(
        0, lens.shape[0], step, (jnp.int32(0), jnp.zeros((8, tok), jnp.int32))
    )
    kpos = start - REACH * tok + lax.broadcasted_iota(jnp.int32, (win, tok), 0)
    ok = (kpos >= first[0:1]) & (kpos <= qpos[0:1])
    once = jnp.where(ok, 0.0, -1e30).astype(F32)
    bias[:, :tok] = once
    bias[:, tok:] = once

    here = pl.ds(pl.multiple_of(run * tok, tok), win)
    k = keys[here, :]
    v = values[here, :]
    for r in range(0, GROUP, 2):
        rows = slice(r * tok, (r + 2) * tok)
        s = dot(k, q[rows], 1, 1) * (SCALE * LOG2E) + bias[...]
        dp = dot(v, do[rows], 1, 1)
        e = jnp.exp2(s - jnp.max(s, axis=0, keepdims=True))
        p = e * (1.0 / jnp.sum(e, axis=0, keepdims=True))
        delta = jnp.sum(p * dp, axis=0, keepdims=True)
        probs[:, rows] = p.astype(BF16)
        dscores[:, rows] = (p * (dp - delta)).astype(BF16)
    gk[here, :] = gk[here, :] + dot(dscores[...], q[...], 1, 0) * SCALE
    gv[here, :] = gv[here, :] + dot(probs[...], do[...], 1, 0)

    @pl.when(o == KVH - 1)
    def _():
        for n in range(REACH):
            back[0, n] = gk[n * tok : (n + 1) * tok].astype(BF16)
            back[1, n] = gv[n * tok : (n + 1) * tok].astype(BF16)
        for n in range(KVH):
            at = slice((REACH + n) * tok, (REACH + n + 1) * tok)
            own[0, n] = gk[at]
            own[1, n] = gv[at]


def attend(where, lens, qs, row, before):
    tok = row.shape[2]
    win, span = (REACH + 1) * tok, (REACH + KVH) * tok
    wide = GROUP * HD

    def whole(*shape):
        return pl.BlockSpec(shape, lambda o: (0,) * len(shape))

    return pl.pallas_call(
        attend_kernel,
        grid=(KVH,),
        in_specs=[SMEM, SMEM]
        + [whole(2, tok, wide)] * KVH
        + [whole(2, KVH, tok, HD), whole(2, REACH, tok, HD)],
        out_specs=[whole(2, REACH, tok, HD), whole(2, KVH, tok, HD)],
        out_shape=[
            jax.ShapeDtypeStruct((2, REACH, tok, HD), BF16),
            jax.ShapeDtypeStruct((2, KVH, tok, HD), F32),
        ],
        scratch_shapes=[
            pltpu.VMEM((GROUP * tok, HD), BF16),
            pltpu.VMEM((GROUP * tok, HD), BF16),
            pltpu.VMEM((span, HD), BF16),
            pltpu.VMEM((span, HD), BF16),
            pltpu.VMEM((span, HD), F32),
            pltpu.VMEM((span, HD), F32),
            pltpu.VMEM((win, 2 * tok), F32),
            pltpu.VMEM((win, GROUP * tok), BF16),
            pltpu.VMEM((win, GROUP * tok), BF16),
        ],
        compiler_params=params(24),
    )(where, lens, *qs, row, before)


def mixing_line(part, grads):
    sums = []
    for i in range(NPHM):
        for a in range(NPHM):
            for b in range(NPHM):
                both = part[a, :, i * HD : (i + 1) * HD] * grads[:, b * HD : (b + 1) * HD]
                sums.append(jnp.sum(both, axis=0, keepdims=True))
    sums = jnp.sum(jnp.concatenate(sums, axis=0), axis=1, keepdims=True)
    many = NPHM**3
    spot = lax.broadcasted_iota(jnp.int32, (many, HD), 0)
    lane = lax.broadcasted_iota(jnp.int32, (many, HD), 1)
    return jnp.sum(jnp.where(spot == lane, sums, 0.0), axis=0, keepdims=True)


def factor_kernel(which, mix, core, *refs):
    xs, g, refs = refs[:8], refs[8], refs[9:]
    (mixed, grads), refs = refs[-2:], refs[:-2]
    tok = g.shape[2]

    @pl.when(pl.program_id(0) == 0)
    def _():
        for b in range(NPHM):
            grads[:tok, b * HD : (b + 1) * HD] = g[core[0], b].astype(F32)
            grads[tok:, b * HD : (b + 1) * HD] = g[1 - core[0], b].astype(F32)
        for a in range(NPHM):
            for n, i in enumerate(which):
                total = mix[i * 16 + a * 4] * grads[:, :HD]
                for b in range(1, NPHM):
                    total = total + mix[i * 16 + a * 4 + b] * grads[:, b * HD : (b + 1) * HD]
                mixed[a, :, n * HD : (n + 1) * HD] = total.astype(BF16)
        if 0 in which:
            line = mixing_line(refs[0], grads)
            line = line + jnp.concatenate([line[:, HD // 2 :], line[:, : HD // 2]], axis=1)
            line = jnp.broadcast_to(split_line(line), (PAD, HD)).astype(BF16)
            for d in range(refs[-1].shape[0]):
                refs[-1][d] = line

    total = None
    for a in range(NPHM):
        x = jnp.concatenate([xs[a][0], xs[NPHM + a][0]], axis=0)
        one = dot(mixed[a], x, 0, 0)
        total = one if total is None else total + one
    outs = refs[1:3] if 0 in which else refs[:2]
    for n, out in enumerate(outs):
        out[...] = total[n * HD : (n + 1) * HD].astype(BF16)


def factor_grads(which, mix, core, xm, xo, g, part=None, n=0):
    tok, width = xm.shape[1:]
    dq, cols = width // NPHM, NPHM * HD
    steps = 4
    ins = [SMEM, SMEM] + chunks(xm, steps) + chunks(xo, steps)
    ins.append(pl.BlockSpec((2, NPHM, tok, HD), lambda j: (0, 0, 0, 0)))
    args = [mix, core] + [xm] * 4 + [xo] * 4 + [g]
    out_specs = [pl.BlockSpec((HD, dq // steps), lambda j: (0, j))] * 2
    out_shape = [jax.ShapeDtypeStruct((HD, dq), BF16)] * 2
    if part is not None:
        ins.append(pl.BlockSpec((NPHM, 2 * tok, cols), lambda j: (0, 0, 0)))
        args.append(part)
        out_specs.append(pl.BlockSpec((n, PAD, HD), lambda j: (0, 0, 0)))
        out_shape.append(jax.ShapeDtypeStruct((n, PAD, HD), BF16))
    return pl.pallas_call(
        functools.partial(factor_kernel, which),
        grid=(steps,),
        in_specs=ins,
        out_specs=out_specs,
        out_shape=out_shape,
        scratch_shapes=[
            pltpu.VMEM((NPHM, 2 * tok, 2 * HD), BF16),
            pltpu.VMEM((2 * tok, cols), F32),
        ],
        compiler_params=params(32),
    )(*args)


def split_line(value):
    lane = lax.broadcasted_iota(jnp.int32, value.shape, 1)
    high = value.astype(BF16).astype(F32)
    return jnp.where(lane < HD // 2, high, value - high)


def turn_kernel(t0, t1, t2, t3, out):
    n, rows = out.shape[:2]
    total = t0[...].astype(F32)
    for t in (t1, t2, t3):
        total = total + t[...].astype(F32)
    turned = total.T.astype(BF16)
    for d in range(n):
        out[d] = turned[d * rows : (d + 1) * rows]


def turn(terms, n):
    rows = terms[0].shape[1] // n
    return pl.pallas_call(
        turn_kernel,
        out_shape=jax.ShapeDtypeStruct((n, rows, HD), BF16),
        compiler_params=params(40),
    )(*terms)


def total_kernel(blocks, lines, out):
    rows = blocks.shape[1]
    total, line = blocks[0].astype(F32), lines[0].astype(F32)
    for d in range(1, blocks.shape[0]):
        total = total + blocks[d].astype(F32)
        line = line + lines[d].astype(F32)
    line = line + jnp.concatenate([line[:, HD // 2 :], line[:, : HD // 2]], axis=1)
    line = split_line(line).astype(BF16)
    body = total.astype(BF16)
    for d in range(out.shape[0]):
        out[d, :rows] = body
        out[d, rows:] = line


def total(blocks, lines, n):
    rows = blocks.shape[1] + PAD
    return pl.pallas_call(
        total_kernel,
        out_shape=jax.ShapeDtypeStruct((n, rows, HD), BF16),
        compiler_params=params(40),
    )(blocks, lines)


def final_kernel(blocks, gk, gv, mk, mv):
    half = NPHM * 2
    rows = gk.shape[0]
    lines = [None, None]
    for i in range(NPHM):
        for c, out in enumerate((gk, gv)):
            at = i * 2 + c
            block = blocks[at].astype(F32)
            for z in range(at + half, blocks.shape[0], half):
                block = block + blocks[z].astype(F32)
            out[:, i, :] = block[:rows]
            line = block[rows : rows + 1]
            lines[c] = line if lines[c] is None else lines[c] + line
    row = lax.broadcasted_iota(jnp.int32, (NPHM, HD), 0)
    lane = lax.broadcasted_iota(jnp.int32, (NPHM, HD), 1)
    col = lax.broadcasted_iota(jnp.int32, (NPHM, NPHM), 1)
    for line, out in zip(lines, (mk, mv)):
        for i in range(NPHM):
            tile = jnp.zeros((NPHM, NPHM), F32)
            for b in range(NPHM):
                mine = (lane & (HD // 2 - 1)) == i * 16 + row * 4 + b
                tile = jnp.where(col == b, jnp.sum(jnp.where(mine, line, 0.0), axis=1, keepdims=True), tile)
            out[i] = tile


def final(blocks, rows):
    return pl.pallas_call(
        final_kernel,
        out_shape=[jax.ShapeDtypeStruct((rows, NPHM, HD), F32)] * 2
        + [jax.ShapeDtypeStruct((NPHM, NPHM, NPHM), F32)] * 2,
        compiler_params=params(40),
    )(blocks)


def shards(inputs, queries, upstream, lengths, factor_k, factor_v, mixing_k, mixing_v):
    tok = inputs.shape[1]
    rows = factor_k.shape[0]
    n_ctx = lax.axis_size("y") * lax.axis_size("zl")
    n_dp = lax.axis_size("zh") * lax.axis_size("x") * lax.axis_size("c")
    z_at = lax.axis_index("zl")
    x_at = lax.axis_index("x")
    first = lax.axis_index("c") == 0
    swap = [(0, 1), (1, 0)]

    other = lax.ppermute(inputs, "c", swap)
    mix = jnp.where(first, mixing_k, mixing_v)
    turned = lax.dynamic_slice_in_dim(jnp.concatenate([mix, mix]), x_at, NPHM, 0).reshape(-1)
    mine = lax.dynamic_index_in_dim(
        jnp.where(first, factor_k, factor_v), x_at, axis=1, keepdims=False
    )
    n_y, n_z = lax.axis_size("y"), lax.axis_size("zl")
    core = lax.axis_index("c").astype(jnp.int32).reshape(1)
    piece = jnp.broadcast_to(mine[None], (n_z, rows, HD))
    wide = GROUP * HD
    blocks = []
    for o in range(KVH):
        head = ((z_at + o) & (KVH - 1)) * wide
        blocks.append(
            jnp.stack([lax.dynamic_slice_in_dim(m[0], head, wide, 1) for m in (queries, upstream)])
        )
    piece = lax.all_to_all(piece, "zl", 0, 0, tiled=True).reshape(1, n_z * rows, HD)
    piece = lax.all_to_all(
        jnp.broadcast_to(piece, (n_y, n_z * rows, HD)), "y", 0, 0, tiled=True
    ).reshape(1, n_ctx * rows, HD)
    q1 = lax.ppermute(blocks[1], "zl", around(1))
    piece, q1, b2 = lax.optimization_barrier((piece, q1, blocks[2]))
    q2 = lax.ppermute(b2, "zl", around(2))
    weights = lax.all_to_all(
        jnp.broadcast_to(piece, (NPHM, n_ctx * rows, HD)), "x", 0, 0, tiled=True
    )
    weights, q2, b3 = lax.optimization_barrier((weights, q2, blocks[3]))
    q3 = lax.ppermute(b3, "zl", around(3))
    part, both = project(mix.reshape(-1), core, inputs, other, weights)

    both, q3 = lax.optimization_barrier((both, q3))
    row = lax.all_to_all(both.reshape(2 * KVH, tok, HD), ("c", "zl"), 0, 0, tiled=True)
    row = row.reshape(2, KVH, tok, HD)
    up = [(n, n + 1) for n in range(lax.axis_size("y") - 1)]
    before = lax.ppermute(row[:, KVH - REACH :], "y", up)
    where = jnp.stack([lax.axis_index("y"), z_at]).astype(jnp.int32)
    back, own = attend(where, lengths[0], [blocks[0], q1, q2, q3], row, before)
    back = lax.ppermute(back, "y", [(n, m) for m, n in up]).astype(F32)
    own = own + jnp.pad(back, ((0, 0), (KVH - REACH, 0), (0, 0), (0, 0)))
    grads = own.astype(BF16).reshape(2 * KVH, tok, HD)
    grads = lax.all_to_all(grads, ("c", "zl"), 0, 0, tiled=True).reshape(2, KVH, tok, HD)

    one, three = factor_grads((1, 3), turned, core, inputs, other, grads)
    sent = [lax.ppermute(one, "x", around(1)), lax.ppermute(three, "x", around(3))]
    own, two, lines = factor_grads((0, 2), turned, core, inputs, other, grads, part, n_ctx)
    sent.append(lax.ppermute(two, "x", around(2)))
    lines = lax.all_to_all(lines, CTX, 0, 0, tiled=True)
    blocks = lax.all_to_all(turn([own] + sent, n_ctx), CTX, 0, 0, tiled=True)
    blocks = lax.all_to_all(total(blocks, lines, n_dp), DP, 0, 0, tiled=True)
    return tuple(final(blocks, rows))


def solution(mesh):
    n_dp, n_ctx = mesh.devices.shape
    zl = 4
    shape = (n_dp // 8, 4, 2, n_ctx // zl, zl)
    wide = Mesh(mesh.devices.reshape(shape), DP + CTX)
    in_specs = (
        P(DP, CTX, None),
        P(DP, CTX, None),
        P(DP, CTX, None),
        P(DP, None),
        P(CTX, None, None),
        P(CTX, None, None),
        P(),
        P(),
    )
    out_specs = (P(CTX, None, None), P(CTX, None, None), P(), P())
    return jax.shard_map(shards, mesh=wide, in_specs=in_specs, out_specs=out_specs, check_vma=False)
```
